256 devices in a mesh: space: 16 (over x_lo, z), snap: 16 (over x_hi, y, core).
Axes of the slice: x: 4 (x_hi: 2, x_lo: 2; x = x_hi * 2 + x_lo), y: 4, z: 8, core: 2. Of those that a mesh axis runs over, the one named last changes fastest.
Arguments:
- snapshots: bfloat16 [1048576, 512], P('space', 'snap'), may hold values from -6 to 6
- mass_blocks: bfloat16 [8192, 3, 128, 128], P(('space', 'snap')), may hold values from -0.3125 to 0.3125
- neighbours: int32 [8192, 3], P(('space', 'snap')), may hold values from 0 to 8191, as said below
- eigvecs: bfloat16 [512, 128], replicated, may hold values from -0.25 to 0.25
Outputs:
- weighted: bfloat16 [1048576, 512], P(('space', 'snap'))
- correlation: float32 [512, 512], P('snap', 'space')
- modes: bfloat16 [1048576, 128], P(('space', 'snap'))
The draws below stay inside these ranges and needn't reach their ends.
Inputs may be any that keep to these rules, and one draw needn't show every extreme that they name: neighbours[b, 0] is b; every entry lies within 4 of b; neighbours[b, 2] lies exactly 4 away from b.
All inputs are finite; a program needn't handle non-finite values.
Results may differ from the reference program's by a relative error of at most 0.0029.
Values may be sent and summed in bfloat16 or wider, within the bound.
No kernel may reach another device: no remote copies, remote signals or barrier semaphores. Data moves between devices by JAX's collectives and lax.ppermute only.
A program may use at most 128 MiB of HBM per device.

```python
import jax
import jax.numpy as jnp
from jax import lax

SNAPS = 512
MODES = 128
BLOCK = 128
NB = 3
HB = 4
NCELLS = 1048576
NBLK = 8192


def draw_neighbours(key, part):
    block_ids = jnp.arange(NBLK, dtype=jnp.int32)
    key_one, key_two, key_three = jax.random.split(key, 3)
    reach_one = jax.random.randint(key_one, (NBLK,), 1, HB + 1, dtype=jnp.int32)
    sign_one = jax.random.randint(key_two, (NBLK,), 0, 2, dtype=jnp.int32) * 2 - 1
    sign_two = jax.random.randint(key_three, (NBLK,), 0, 2, dtype=jnp.int32) * 2 - 1

    def mirror(reach, sign):
        target = block_ids + sign * reach
        outside = (target < 0) | (target >= NBLK)
        return jnp.where(outside, block_ids - sign * reach, target)
    far_reach = jnp.full((NBLK,), HB, dtype=jnp.int32)
    return jnp.stack([block_ids, mirror(reach_one, sign_one), mirror(far_reach, sign_two)], axis=1).astype(jnp.int32)


def block_levels(stream_key, extent, cuts, smallest, largest):
    level, own = 1.0, jax.random.fold_in(stream_key, 6)
    for position, blocks in cuts:
        draws = jnp.exp(jax.random.uniform(jax.random.fold_in(own, position), (blocks,), jnp.float32, smallest / len(cuts), largest / len(cuts)))
        level = level * jnp.repeat(draws, extent[position] // blocks).reshape([-1 if axis == position else 1 for axis in range(len(extent))])
    return level


def bell_draw(rng, dims, spread, bound, cuts=(), kind=jnp.bfloat16):
    result = spread * jax.random.normal(rng, dims, jnp.float32)
    if cuts:
        result = result * block_levels(rng, dims, cuts, -0.22, 0.18)
    return jnp.clip(result, -bound, bound).astype(kind)


def setup_inputs(seed: int = 0) -> dict:
    seeds = jax.random.split(jax.random.key(seed), 5)
    snapshots = bell_draw(seeds[0], (NCELLS, SNAPS), 1.0, 6.0, ((0, 16), (1, 16)))
    mass_blocks = bell_draw(seeds[1], (NBLK, NB, BLOCK, BLOCK), (NB * BLOCK) ** -0.5, 0.3125, ((0, 256),))
    neighbours = draw_neighbours(jax.random.fold_in(seeds[4], 71), 0)
    eigvecs = bell_draw(seeds[3], (SNAPS, MODES), SNAPS ** -0.5, 0.25)
    return dict(snapshots=snapshots, mass_blocks=mass_blocks, neighbours=neighbours, eigvecs=eigvecs)


group_size = 32


def reference(snapshots, mass_blocks, neighbours, eigvecs):
    blocks = snapshots.reshape(NBLK, BLOCK, SNAPS)

    def weigh(packed):
        mass_part, block_ids = packed
        nearby = blocks[block_ids].astype(jnp.float32)
        return jnp.einsum("bjrc,bjcs->brs", mass_part.astype(jnp.float32), nearby)

    stacked = lax.map(weigh, (mass_blocks.reshape(-1, group_size, NB, BLOCK, BLOCK), neighbours.reshape(-1, group_size, NB)))
    weighted = stacked.reshape(NCELLS, SNAPS).astype(jnp.bfloat16)
    correlation = jnp.dot(weighted.T, snapshots, preferred_element_type=jnp.float32) * (1.0 / NCELLS)
    modes = jnp.dot(snapshots, eigvecs, preferred_element_type=jnp.float32).astype(jnp.bfloat16)
    return weighted, correlation, modes
```

```python
import jax
import jax.numpy as jnp
from jax import lax
from jax.experimental import pallas as pl
from jax.experimental.pallas import tpu as pltpu
from jax.sharding import PartitionSpec as P

HB = 4
STEP = 4
AXES = ("space", "snap")
MIB = 1 << 20


def contract(a, b, dim_a, dim_b):
    return lax.dot_general(a, b, (((dim_a,), (dim_b,)), ((), ())), preferred_element_type=jnp.float32)


def weigh(place, blocks, mass_ref, field_ref, weighted_ref, size):
    for k in range(blocks):
        near = [field_ref[:, pl.ds(pl.multiple_of(place(k, j) * size, size), size)] for j in range(3)]
        mass = [mass_ref[k, j] for j in range(3)]
        block = contract(jnp.concatenate(mass, axis=1), jnp.concatenate(near, axis=1), 1, 1)
        weighted_ref[k * size : (k + 1) * size, :] = block.astype(weighted_ref.dtype)


def interior_kernel(where_ref, neighbours_ref, field_ref, mass_ref, weighted_ref, corr_ref):
    step = pl.program_id(0)
    size = mass_ref.shape[2]

    def place(k, j):
        return neighbours_ref[j, (step + 1) * STEP + k] - where_ref[0]

    @pl.when(step == 0)
    def _():
        corr_ref[...] = jnp.zeros_like(corr_ref)

    weigh(place, STEP, mass_ref, field_ref, weighted_ref, size)
    width = STEP * size
    own = field_ref[:, pl.ds(pl.multiple_of((step + 1) * width, width), width)]
    corr_ref[...] += contract(own, weighted_ref[...], 1, 0)


def rim_kernel(where_ref, neighbours_ref, field_ref, below_ref, above_ref, mass_ref, corr_in_ref, _, weighted_ref,
               keep_ref, send_ref, extended, corr):
    step = pl.program_id(0)
    size = mass_ref.shape[2]
    width = STEP * size
    count = neighbours_ref.shape[1]
    first = step * (count - STEP)

    def place(k, j):
        return neighbours_ref[j, first + k] - where_ref[0] - first + HB

    @pl.when(step == 0)
    def _():
        corr[...] = corr_in_ref[...]
        extended[:, :width] = below_ref[...]
        extended[:, width:] = field_ref[...]

    @pl.when(step == 1)
    def _():
        extended[:, : 2 * width] = field_ref[...]
        extended[:, 2 * width :] = above_ref[...]

    weigh(place, STEP, mass_ref, extended, weighted_ref, size)
    corr[...] += contract(extended[:, width : 2 * width], weighted_ref[...], 1, 0)

    @pl.when(step == 1)
    def _():
        corr[...] = corr[...].T
        core = where_ref[1]
        tile = keep_ref.shape[1]
        for k in range(keep_ref.shape[0]):
            keep_ref[k] = corr[pl.ds(pl.multiple_of((2 * k + core) * tile, tile), tile), :]
            send_ref[k] = corr[pl.ds(pl.multiple_of((2 * k + 1 - core) * tile, tile), tile), :]


def modes_kernel(field_ref, vectors_ref, modes_ref):
    modes_ref[...] = contract(vectors_ref[...], field_ref[...], 0, 0).T.astype(modes_ref.dtype)


def flipped(value, mask):
    return lax.ppermute(value, AXES, [(i, i ^ mask) for i in range(lax.axis_size(AXES))])


def shifted(value, distance):
    count = lax.axis_size(AXES)
    return lax.ppermute(value, AXES, [(i, (i + distance) % count) for i in range(count)])


def shards(snapshots, mass_blocks, neighbours, eigvecs):
    cells, mine = snapshots.shape
    group = lax.axis_size("snap")
    spaces = lax.axis_size("space")
    rows = cells // group
    snaps = mine * group
    count, _, size, _ = mass_blocks.shape
    width = STEP * size
    modes_count = eigvecs.shape[1]

    parts = snapshots.T.reshape(mine, group, rows).transpose(1, 0, 2)
    field = lax.all_to_all(parts, "snap", split_axis=0, concat_axis=0).reshape(snaps, rows)
    below = shifted(field[:, rows - width :], 1)
    above = shifted(field[:, :width], -1)

    where = jnp.stack([lax.axis_index(AXES) * count, lax.axis_index("snap") & 1]).astype(jnp.int32)
    listed = neighbours.T
    scalar = pl.BlockSpec(memory_space=pltpu.SMEM)
    inner = count // STEP - 2
    weighted, corr = pl.pallas_call(
        interior_kernel,
        grid=(inner,),
        in_specs=[
            scalar,
            scalar,
            pl.BlockSpec((snaps, rows), lambda i: (0, 0)),
            pl.BlockSpec((STEP, 3, size, size), lambda i: (i + 1, 0, 0, 0)),
        ],
        out_specs=[
            pl.BlockSpec((width, snaps), lambda i: (i + 1, 0)),
            pl.BlockSpec((snaps, snaps), lambda i: (0, 0)),
        ],
        out_shape=[
            jax.ShapeDtypeStruct((rows, snaps), jnp.bfloat16),
            jax.ShapeDtypeStruct((snaps, snaps), jnp.float32),
        ],
        compiler_params=pltpu.CompilerParams(vmem_limit_bytes=28 * MIB),
        cost_estimate=pl.CostEstimate(flops=inner * 2 * width * snaps * (3 * size + snaps), bytes_accessed=12 * MIB, transcendentals=0),
        name="interior",
    )(where, listed, field, mass_blocks)

    last = rows // (2 * width) - 1
    weighted, keep, send = pl.pallas_call(
        rim_kernel,
        grid=(2,),
        in_specs=[
            scalar,
            scalar,
            pl.BlockSpec((snaps, 2 * width), lambda i: (0, i * last)),
            pl.BlockSpec((snaps, width), lambda i: (0, 0)),
            pl.BlockSpec((snaps, width), lambda i: (0, 0)),
            pl.BlockSpec((STEP, 3, size, size), lambda i: (i * (inner + 1), 0, 0, 0)),
            pl.BlockSpec((snaps, snaps), lambda i: (0, 0)),
            pl.BlockSpec(memory_space=pl.ANY),
        ],
        out_specs=[
            pl.BlockSpec((width, snaps), lambda i: (i * (inner + 1), 0)),
            pl.BlockSpec((group // 2, mine, snaps), lambda i: (0, 0, 0)),
            pl.BlockSpec((group // 2, mine, snaps), lambda i: (0, 0, 0)),
        ],
        out_shape=[
            jax.ShapeDtypeStruct((rows, snaps), jnp.bfloat16),
            jax.ShapeDtypeStruct((group // 2, mine, snaps), jnp.float32),
            jax.ShapeDtypeStruct((group // 2, mine, snaps), jnp.float32),
        ],
        scratch_shapes=[pltpu.VMEM((snaps, 3 * width), jnp.bfloat16), pltpu.VMEM((snaps, snaps), jnp.float32)],
        input_output_aliases={7: 0},
        compiler_params=pltpu.CompilerParams(vmem_limit_bytes=28 * MIB),
        cost_estimate=pl.CostEstimate(flops=4 * width * snaps * (3 * size + snaps), bytes_accessed=8 * MIB, transcendentals=0),
        name="rim",
    )(where, listed, field, below, above, mass_blocks, corr, weighted)

    summed = keep + flipped(send, 1)
    chips = [[2 * k + core for k in range(group // 2)] for core in range(2)]
    summed = lax.all_to_all(summed, "snap", split_axis=0, concat_axis=0, axis_index_groups=chips).sum(0)
    tiles = summed.reshape(mine, spaces, snaps // spaces).transpose(1, 0, 2)
    correlation = lax.all_to_all(tiles, "space", split_axis=0, concat_axis=0).sum(0)
    correlation = correlation * (1.0 / (rows * lax.axis_size(AXES)))

    modes = pl.pallas_call(
        modes_kernel,
        grid=(rows // 1024,),
        in_specs=[
            pl.BlockSpec((snaps, 1024), lambda i: (0, i)),
            pl.BlockSpec((snaps, modes_count), lambda i: (0, 0)),
        ],
        out_specs=pl.BlockSpec((1024, modes_count), lambda i: (i, 0)),
        out_shape=jax.ShapeDtypeStruct((rows, modes_count), jnp.bfloat16),
        compiler_params=pltpu.CompilerParams(vmem_limit_bytes=16 * MIB),
        cost_estimate=pl.CostEstimate(flops=2 * rows * snaps * modes_count, bytes_accessed=5 * MIB, transcendentals=0),
        name="modes",
    )(field, eigvecs)
    return weighted, correlation, modes


def solution(mesh):
    in_specs = (
        P("space", "snap"),
        P(AXES, None, None, None),
        P(AXES, None),
        P(),
    )
    out_specs = (P(AXES, None), P("snap", "space"), P(AXES, None))
    return jax.shard_map(shards, mesh=mesh, in_specs=in_specs, out_specs=out_specs, check_vma=False)
```

```python
import functools

import jax
import jax.numpy as jnp
from jax import lax
from jax.experimental import pallas as pl
from jax.experimental.pallas import tpu as pltpu
from jax.sharding import PartitionSpec as P

HB = 4
STEP = 4
AXES = ("space", "snap")
MIB = 1 << 20


def contract(a, b, dim_a, dim_b):
    return lax.dot_general(a, b, (((dim_a,), (dim_b,)), ((), ())), preferred_element_type=jnp.float32)


def weigh(place, blocks, mass_ref, field_ref, weighted_ref, size):
    for k in range(blocks):
        near = [field_ref[:, pl.ds(pl.multiple_of(place(k, j) * size, size), size)] for j in range(3)]
        mass = [mass_ref[k, j] for j in range(3)]
        block = contract(jnp.concatenate(mass, axis=1), jnp.concatenate(near, axis=1), 1, 1)
        weighted_ref[k * size : (k + 1) * size, :] = block.astype(weighted_ref.dtype)


def here():
    snap = lax.axis_index("snap")
    return lax.axis_index("space") * lax.axis_size("snap") + snap, lax.rem(snap, 2)


def chunks_kernel(field_ref, parts_ref, sems):
    group, _, length = parts_ref.shape
    own = field_ref.shape[1] // group
    halo = length - own
    copies = []
    for k in range(group):
        start, to, size = k * own - (1 - k % 2) * halo, 0, length
        if k == 0:
            start, to, size = 0, halo, own
        if k == group - 1:
            size = own
        source = field_ref.at[:, pl.ds(start, size)]
        copies.append(pltpu.make_async_copy(source, parts_ref.at[k, :, pl.ds(to, size)], sems.at[k]))
        copies[-1].start()
    for copy in copies:
        copy.wait()


def ends_kernel(before_ref, after_ref, parts_in_ref, parts_ref, sems):
    del parts_in_ref
    group, _, length = parts_ref.shape
    halo = before_ref.shape[1]
    copies = [
        pltpu.make_async_copy(before_ref, parts_ref.at[0, :, pl.ds(0, halo)], sems.at[0]),
        pltpu.make_async_copy(after_ref, parts_ref.at[group - 1, :, pl.ds(length - halo, halo)], sems.at[1]),
    ]
    for copy in copies:
        copy.start()
    for copy in copies:
        copy.wait()


def inner_kernel(neighbours_ref, field_ref, mass_ref, weighted_ref, corr_ref, copy_ref, edge_ref, next_ref, block,
                 block_sems, copy_sem):
    count, _, size, _ = mass_ref.shape
    width = STEP * size
    groups = count // STEP
    device, core = here()
    shift = device * count - (1 - core) * STEP
    own = pl.ds(pl.multiple_of((1 - core) * width, width), count * size)
    copy = pltpu.make_async_copy(field_ref.at[:, own], copy_ref, copy_sem)
    copy.start()
    edge_ref[...] = field_ref[:, pl.ds(pl.multiple_of((1 - core) * groups * width, width), width)]
    next_ref[...] = field_ref[:, pl.ds(pl.multiple_of(core * width + (1 - core) * (groups - 1) * width, width), width)]
    writes = []
    for step in range(groups - 1):
        slot = step % 2
        if len(writes) >= 2:
            writes[-2].wait()
        first = (step + core) * STEP

        def place(k, j):
            return neighbours_ref[j, first + k] - shift

        weigh(place, STEP, mass_ref.at[pl.ds(first, STEP)], field_ref, block.at[slot], size)
        rows = pl.ds(pl.multiple_of(first * size, width), width)
        writes.append(pltpu.make_async_copy(block.at[slot], weighted_ref.at[rows], block_sems.at[slot]))
        writes[-1].start()
        term = contract(field_ref[:, (step + 1) * width : (step + 2) * width], block[slot], 1, 0)
        corr_ref[...] = term if step == 0 else corr_ref[...] + term
    writes[-2].wait()
    writes[-1].wait()
    copy.wait()


def edge_kernel(neighbours_ref, edge_ref, next_ref, near_ref, mass_ref, corr_in_ref, weighted_in_ref, weighted_ref,
                keep_ref, send_ref, extended, block, block_sem, corr):
    del weighted_in_ref
    count, _, size, _ = mass_ref.shape
    width = STEP * size
    device, core = here()
    first = (1 - core) * (count - STEP)
    extended[:, width : 2 * width] = edge_ref[...]

    @pl.when(core == 0)
    def _():
        extended[:, :width] = next_ref[...]
        extended[:, 2 * width :] = near_ref[...]

    @pl.when(core != 0)
    def _():
        extended[:, :width] = near_ref[...]
        extended[:, 2 * width :] = next_ref[...]

    def place(k, j):
        return neighbours_ref[j, first + k] - device * count - first + HB

    weigh(place, STEP, mass_ref.at[pl.ds(first, STEP)], extended, block, size)
    rows = pl.ds(pl.multiple_of(first * size, width), width)
    write = pltpu.make_async_copy(block, weighted_ref.at[rows], block_sem)
    write.start()
    corr[...] = (corr_in_ref[...] + contract(edge_ref[...], block[...], 1, 0)).T
    tile = keep_ref.shape[1]
    for k in range(keep_ref.shape[0]):
        keep_ref[k] = corr[pl.ds(pl.multiple_of((2 * k + core) * tile, tile), tile), :]
        send_ref[k] = corr[pl.ds(pl.multiple_of((2 * k + 1 - core) * tile, tile), tile), :]
    write.wait()


def pack_kernel(parts_ref, packed_ref):
    total = parts_ref[0]
    for k in range(1, parts_ref.shape[0]):
        total = total + parts_ref[k]
    high, lanes = packed_ref.shape[1:]
    tile = total.shape[0]
    share = lanes // tile
    group = lax.broadcasted_iota(jnp.int32, (high, lanes), 1) // tile
    for k in range(packed_ref.shape[0]):
        piece = total[:, k // share * lanes : (k // share + 1) * lanes]
        packed = jnp.zeros((high, lanes), jnp.float32)
        for g in range(share):
            moved = piece[g * high : (g + 1) * high]
            turn = (g - k % share) % share * tile
            if turn:
                moved = pltpu.roll(moved, turn, 1)
            packed = jnp.where(group == g, moved, packed)
        packed_ref[k] = packed


def unpack_kernel(scale, packed_ref, tile_ref):
    total = packed_ref[0]
    for k in range(1, packed_ref.shape[0]):
        total = total + packed_ref[k]
    total = total * scale
    high = packed_ref.shape[1]
    tile = tile_ref.shape[1]
    share = packed_ref.shape[2] // tile
    for g in range(share):
        tile_ref[g * high : (g + 1) * high, :] = total[:, g * tile : (g + 1) * tile]


def modes_kernel(field_ref, vectors_ref, modes_ref):
    modes_ref[...] = contract(vectors_ref[...], field_ref[...], 0, 0).T.astype(modes_ref.dtype)


def flipped(value, mask):
    return lax.ppermute(value, AXES, [(i, i ^ mask) for i in range(lax.axis_size(AXES))])


def shifted(value, axis, distance):
    count = lax.axis_size(axis)
    return lax.ppermute(value, axis, [(i, (i + distance) % count) for i in range(count)])


def call(kernel, name, operands, out_shape, moved, flops=0, apart=(), out_apart=(), scratch=(), limit=24, **more):
    vmem, smem, anywhere = (pl.BlockSpec(memory_space=m) for m in (pltpu.VMEM, pltpu.SMEM, pl.ANY))
    specs = [smem if x.dtype == jnp.int32 else anywhere if k in apart else vmem for k, x in enumerate(operands)]
    return pl.pallas_call(
        kernel,
        in_specs=specs,
        out_specs=[anywhere if k in out_apart else vmem for k in range(len(out_shape))],
        out_shape=out_shape,
        scratch_shapes=scratch,
        compiler_params=pltpu.CompilerParams(vmem_limit_bytes=limit * MIB),
        cost_estimate=pl.CostEstimate(flops=flops, bytes_accessed=moved, transcendentals=0),
        name=name,
        **more,
    )(*operands)


def shards(snapshots, mass_blocks, neighbours, eigvecs):
    cells, mine = snapshots.shape
    group = lax.axis_size("snap")
    spaces = lax.axis_size("space")
    rows = cells // group
    snaps = mine * group
    size = mass_blocks.shape[2]
    width = STEP * size
    modes_count = eigvecs.shape[1]

    def half(*dims):
        return jax.ShapeDtypeStruct(dims, jnp.bfloat16)

    def single(*dims):
        return jax.ShapeDtypeStruct(dims, jnp.float32)

    sems = pltpu.SemaphoreType.DMA
    flat = snapshots.T
    before = shifted(flat[:, cells - width :], "space", 1)
    after = shifted(flat[:, :width], "space", -1)
    chunked = [half(group, mine, rows + width)]
    (parts,) = call(
        chunks_kernel, "chunks", (flat,), chunked, 8 * MIB, apart=(0,), out_apart=(0,), scratch=[sems((group,))]
    )
    (parts,) = call(
        ends_kernel,
        "ends",
        (before, after, parts),
        chunked,
        MIB // 16,
        apart=(0, 1, 2),
        out_apart=(0,),
        scratch=[sems((2,))],
        input_output_aliases={2: 0},
    )
    field = lax.all_to_all(parts, "snap", split_axis=0, concat_axis=0).reshape(snaps, rows + width)
    listed = neighbours.T
    per_row = 2 * snaps * (3 * size + snaps)
    weighted, corr, field, edge, following = call(
        inner_kernel,
        "inner",
        (listed, field, mass_blocks),
        [half(rows, snaps), single(snaps, snaps), half(snaps, rows)] + [half(snaps, width)] * 2,
        14 * MIB,
        (rows - width) * per_row,
        out_apart=(0, 2),
        scratch=[pltpu.VMEM((2, width, snaps), jnp.bfloat16), sems((2,)), sems(())],
    )
    near = flipped(edge, 1)
    modes = pl.pallas_call(
        modes_kernel,
        grid=(rows // 1024,),
        in_specs=[
            pl.BlockSpec((snaps, 1024), lambda i: (0, i)),
            pl.BlockSpec((snaps, modes_count), lambda i: (0, 0)),
        ],
        out_specs=pl.BlockSpec((1024, modes_count), lambda i: (i, 0)),
        out_shape=half(rows, modes_count),
        compiler_params=pltpu.CompilerParams(vmem_limit_bytes=16 * MIB),
        cost_estimate=pl.CostEstimate(flops=2 * rows * snaps * modes_count, bytes_accessed=5 * MIB, transcendentals=0),
        name="modes",
    )(field, eigvecs)
    weighted, keep, send = call(
        edge_kernel,
        "edge",
        (listed, edge, following, near, mass_blocks, corr, weighted),
        [half(rows, snaps)] + [single(group // 2, mine, snaps)] * 2,
        6 * MIB,
        width * per_row,
        apart=(6,),
        out_apart=(0,),
        scratch=[
            pltpu.VMEM((snaps, 3 * width), jnp.bfloat16),
            pltpu.VMEM((width, snaps), jnp.bfloat16),
            sems(()),
            pltpu.VMEM((snaps, snaps), jnp.float32),
        ],
        input_output_aliases={6: 0},
    )

    summed = keep + flipped(send, 1)
    chips = [[2 * k + core for k in range(group // 2)] for core in range(2)]
    summed = lax.all_to_all(summed, "snap", split_axis=0, concat_axis=0, axis_index_groups=chips)
    tile = snaps // spaces
    (packed,) = call(pack_kernel, "pack", (summed,), [single(spaces, mine * tile // 128, 128)], MIB)
    packed = lax.all_to_all(packed, "space", split_axis=0, concat_axis=0)
    scale = 1.0 / (rows * lax.axis_size(AXES))
    (correlation,) = call(functools.partial(unpack_kernel, scale), "unpack", (packed,), [single(mine, tile)], MIB)
    return weighted, correlation, modes


def solution(mesh):
    in_specs = (
        P("space", "snap"),
        P(AXES, None, None, None),
        P(AXES, None),
        P(),
    )
    out_specs = (P(AXES, None), P("snap", "space"), P(AXES, None))
    return jax.shard_map(shards, mesh=mesh, in_specs=in_specs, out_specs=out_specs, check_vma=False)
```

```python
import functools

import jax
import jax.numpy as jnp
from jax import lax
from jax.experimental import pallas as pl
from jax.experimental.pallas import tpu as pltpu
from jax.sharding import PartitionSpec as P

HB = 4
STEP = 4
AXES = ("space", "snap")
MIB = 1 << 20


def contract(a, b, dim_a, dim_b):
    return lax.dot_general(a, b, (((dim_a,), (dim_b,)), ((), ())), preferred_element_type=jnp.float32)


def weigh(place, blocks, mass_ref, field_ref, weighted_ref, size):
    for k in range(blocks):
        near = [field_ref[:, pl.ds(pl.multiple_of(place(k, j) * size, size), size)] for j in range(3)]
        block = sum(contract(mass_ref[k, j], near[j], 1, 1) for j in range(3))
        weighted_ref[k * size : (k + 1) * size, :] = block.astype(weighted_ref.dtype)


def here():
    snap = lax.axis_index("snap")
    return lax.axis_index("space") * lax.axis_size("snap") + snap, lax.rem(snap, 2)


def chunks_kernel(field_ref, parts_ref, sems):
    group, _, length = parts_ref.shape
    own = field_ref.shape[1] // group
    halo = length - own
    copies = []
    for k in range(group):
        start, to, size = k * own - (1 - k % 2) * halo, 0, length
        if k == 0:
            start, to, size = 0, halo, own
        if k == group - 1:
            size = own
        source = field_ref.at[:, pl.ds(start, size)]
        copies.append(pltpu.make_async_copy(source, parts_ref.at[k, :, pl.ds(to, size)], sems.at[k]))
        copies[-1].start()
    for copy in copies:
        copy.wait()


def ends_kernel(before_ref, after_ref, parts_in_ref, parts_ref, sems):
    del parts_in_ref
    group, _, length = parts_ref.shape
    halo = before_ref.shape[1]
    copies = [
        pltpu.make_async_copy(before_ref, parts_ref.at[0, :, pl.ds(0, halo)], sems.at[0]),
        pltpu.make_async_copy(after_ref, parts_ref.at[group - 1, :, pl.ds(length - halo, halo)], sems.at[1]),
    ]
    for copy in copies:
        copy.start()
    for copy in copies:
        copy.wait()


def cut_kernel(field_ref, mass_ref, edge_ref):
    del mass_ref
    width = edge_ref.shape[1]
    core = here()[1]
    edge_ref[...] = field_ref[:, pl.ds(pl.multiple_of((1 - core) * (field_ref.shape[1] - width), width), width)]


def inner_kernel(neighbours_ref, field_ref, mass_ref, weighted_ref, corr_ref, copy_ref, next_ref, block,
                 block_sems, copy_sem):
    count, _, size, _ = mass_ref.shape
    width = STEP * size
    groups = count // STEP
    device, core = here()
    shift = device * count - (1 - core) * STEP
    own = pl.ds(pl.multiple_of((1 - core) * width, width), count * size)
    copy = pltpu.make_async_copy(field_ref.at[:, own], copy_ref, copy_sem)
    copy.start()
    next_ref[...] = field_ref[:, pl.ds(pl.multiple_of(core * width + (1 - core) * (groups - 1) * width, width), width)]
    writes = []
    for step in range(groups - 1):
        slot = step % 2
        if len(writes) >= 2:
            writes[-2].wait()
        first = (step + core) * STEP

        def place(k, j):
            return neighbours_ref[j, first + k] - shift

        weigh(place, STEP, mass_ref.at[pl.ds(first, STEP)], field_ref, block.at[slot], size)
        rows = pl.ds(pl.multiple_of(first * size, width), width)
        writes.append(pltpu.make_async_copy(block.at[slot], weighted_ref.at[rows], block_sems.at[slot]))
        writes[-1].start()
        term = contract(field_ref[:, (step + 1) * width : (step + 2) * width], block[slot], 1, 0)
        corr_ref[...] = term if step == 0 else corr_ref[...] + term
    writes[-2].wait()
    writes[-1].wait()
    copy.wait()


def edge_kernel(neighbours_ref, edge_ref, next_ref, near_ref, mass_ref, corr_in_ref, weighted_in_ref, weighted_ref,
                keep_ref, send_ref, extended, block, block_sem, corr):
    del weighted_in_ref
    count, _, size, _ = mass_ref.shape
    width = STEP * size
    device, core = here()
    first = (1 - core) * (count - STEP)
    extended[:, width : 2 * width] = edge_ref[...]

    @pl.when(core == 0)
    def _():
        extended[:, :width] = next_ref[...]
        extended[:, 2 * width :] = near_ref[...]

    @pl.when(core != 0)
    def _():
        extended[:, :width] = near_ref[...]
        extended[:, 2 * width :] = next_ref[...]

    def place(k, j):
        return neighbours_ref[j, first + k] - device * count - first + HB

    weigh(place, STEP, mass_ref.at[pl.ds(first, STEP)], extended, block, size)
    rows = pl.ds(pl.multiple_of(first * size, width), width)
    write = pltpu.make_async_copy(block, weighted_ref.at[rows], block_sem)
    write.start()
    corr[...] = (corr_in_ref[...] + contract(edge_ref[...], block[...], 1, 0)).T
    tile = keep_ref.shape[1]
    for k in range(keep_ref.shape[0]):
        keep_ref[k] = corr[pl.ds(pl.multiple_of((2 * k + core) * tile, tile), tile), :]
        send_ref[k] = corr[pl.ds(pl.multiple_of((2 * k + 1 - core) * tile, tile), tile), :]
    write.wait()


def pack_kernel(parts_ref, packed_ref):
    total = parts_ref[0]
    for k in range(1, parts_ref.shape[0]):
        total = total + parts_ref[k]
    high, lanes = packed_ref.shape[1:]
    tile = total.shape[0]
    share = lanes // tile
    group = lax.broadcasted_iota(jnp.int32, (high, lanes), 1) // tile
    for k in range(packed_ref.shape[0]):
        piece = total[:, k // share * lanes : (k // share + 1) * lanes]
        packed = jnp.zeros((high, lanes), jnp.float32)
        for g in range(share):
            moved = piece[g * high : (g + 1) * high]
            turn = (g - k % share) % share * tile
            if turn:
                moved = pltpu.roll(moved, turn, 1)
            packed = jnp.where(group == g, moved, packed)
        packed_ref[k] = packed


def unpack_kernel(scale, packed_ref, tile_ref):
    total = packed_ref[0]
    for k in range(1, packed_ref.shape[0]):
        total = total + packed_ref[k]
    total = total * scale
    high = packed_ref.shape[1]
    tile = tile_ref.shape[1]
    share = packed_ref.shape[2] // tile
    for g in range(share):
        tile_ref[g * high : (g + 1) * high, :] = total[:, g * tile : (g + 1) * tile]


def modes_kernel(field_ref, vectors_ref, modes_ref):
    modes_ref[...] = contract(vectors_ref[...], field_ref[...], 0, 0).T.astype(modes_ref.dtype)


def flipped(value, mask):
    return lax.ppermute(value, AXES, [(i, i ^ mask) for i in range(lax.axis_size(AXES))])


def shifted(value, axis, distance):
    count = lax.axis_size(axis)
    return lax.ppermute(value, axis, [(i, (i + distance) % count) for i in range(count)])


def call(kernel, name, operands, out_shape, moved, flops=0, apart=(), out_apart=(), scratch=(), limit=24, **more):
    vmem, smem, anywhere = (pl.BlockSpec(memory_space=m) for m in (pltpu.VMEM, pltpu.SMEM, pl.ANY))
    specs = [smem if x.dtype == jnp.int32 else anywhere if k in apart else vmem for k, x in enumerate(operands)]
    return pl.pallas_call(
        kernel,
        in_specs=specs,
        out_specs=[anywhere if k in out_apart else vmem for k in range(len(out_shape))],
        out_shape=out_shape,
        scratch_shapes=scratch,
        compiler_params=pltpu.CompilerParams(vmem_limit_bytes=limit * MIB),
        cost_estimate=pl.CostEstimate(flops=flops, bytes_accessed=moved, transcendentals=0),
        name=name,
        **more,
    )(*operands)


def shards(snapshots, mass_blocks, neighbours, eigvecs):
    cells, mine = snapshots.shape
    group = lax.axis_size("snap")
    spaces = lax.axis_size("space")
    rows = cells // group
    snaps = mine * group
    size = mass_blocks.shape[2]
    width = STEP * size
    modes_count = eigvecs.shape[1]

    def half(*dims):
        return jax.ShapeDtypeStruct(dims, jnp.bfloat16)

    def single(*dims):
        return jax.ShapeDtypeStruct(dims, jnp.float32)

    sems = pltpu.SemaphoreType.DMA
    flat = snapshots.T
    before = shifted(flat[:, cells - width :], "space", 1)
    after = shifted(flat[:, :width], "space", -1)
    chunked = [half(group, mine, rows + width)]
    (parts,) = call(
        chunks_kernel, "chunks", (flat,), chunked, 8 * MIB, apart=(0,), out_apart=(0,), scratch=[sems((group,))]
    )
    (parts,) = call(
        ends_kernel,
        "ends",
        (before, after, parts),
        chunked,
        MIB // 16,
        apart=(0, 1, 2),
        out_apart=(0,),
        scratch=[sems((2,))],
        input_output_aliases={2: 0},
    )
    field = lax.all_to_all(parts, "snap", split_axis=0, concat_axis=0).reshape(snaps, rows + width)
    listed = neighbours.T
    per_row = 2 * snaps * (3 * size + snaps)
    (edge,) = call(cut_kernel, "cut", (field, mass_blocks), [half(snaps, width)], MIB)
    near = flipped(edge, 1)
    weighted, corr, field, following = call(
        inner_kernel,
        "inner",
        (listed, field, mass_blocks),
        [half(rows, snaps), single(snaps, snaps), half(snaps, rows)] + [half(snaps, width)],
        14 * MIB,
        (rows - width) * per_row,
        out_apart=(0, 2),
        scratch=[pltpu.VMEM((2, width, snaps), jnp.bfloat16), sems((2,)), sems(())],
    )
    modes = pl.pallas_call(
        modes_kernel,
        grid=(rows // 1024,),
        in_specs=[
            pl.BlockSpec((snaps, 1024), lambda i: (0, i)),
            pl.BlockSpec((snaps, modes_count), lambda i: (0, 0)),
        ],
        out_specs=pl.BlockSpec((1024, modes_count), lambda i: (i, 0)),
        out_shape=half(rows, modes_count),
        compiler_params=pltpu.CompilerParams(vmem_limit_bytes=16 * MIB),
        cost_estimate=pl.CostEstimate(flops=2 * rows * snaps * modes_count, bytes_accessed=5 * MIB, transcendentals=0),
        name="modes",
    )(field, eigvecs)
    weighted, keep, send = call(
        edge_kernel,
        "edge",
        (listed, edge, following, near, mass_blocks, corr, weighted),
        [half(rows, snaps)] + [single(group // 2, mine, snaps)] * 2,
        6 * MIB,
        width * per_row,
        apart=(6,),
        out_apart=(0,),
        scratch=[
            pltpu.VMEM((snaps, 3 * width), jnp.bfloat16),
            pltpu.VMEM((width, snaps), jnp.bfloat16),
            sems(()),
            pltpu.VMEM((snaps, snaps), jnp.float32),
        ],
        input_output_aliases={6: 0},
    )

    summed = keep + flipped(send, 1)
    chips = [[2 * k + core for k in range(group // 2)] for core in range(2)]
    summed = lax.all_to_all(summed, "snap", split_axis=0, concat_axis=0, axis_index_groups=chips)
    tile = snaps // spaces
    (packed,) = call(pack_kernel, "pack", (summed,), [single(spaces, mine * tile // 128, 128)], MIB)
    packed = lax.all_to_all(packed, "space", split_axis=0, concat_axis=0)
    scale = 1.0 / (rows * lax.axis_size(AXES))
    (correlation,) = call(functools.partial(unpack_kernel, scale), "unpack", (packed,), [single(mine, tile)], MIB)
    return weighted, correlation, modes


def solution(mesh):
    in_specs = (
        P("space", "snap"),
        P(AXES, None, None, None),
        P(AXES, None),
        P(),
    )
    out_specs = (P(AXES, None), P("snap", "space"), P(AXES, None))
    return jax.shard_map(shards, mesh=mesh, in_specs=in_specs, out_specs=out_specs, check_vma=False)
```

```python
import functools

import jax
import jax.numpy as jnp
from jax import lax
from jax.experimental import pallas as pl
from jax.experimental.pallas import tpu as pltpu
from jax.sharding import PartitionSpec as P

HB = 4
STEP = 4
AXES = ("space", "snap")
MIB = 1 << 20


def contract(a, b, dim_a, dim_b):
    return lax.dot_general(a, b, (((dim_a,), (dim_b,)), ((), ())), preferred_element_type=jnp.float32)


def weigh(place, blocks, mass_ref, field_ref, weighted_ref, size):
    for k in range(blocks):
        near = [field_ref[:, pl.ds(pl.multiple_of(place(k, j) * size, size), size)] for j in range(3)]
        block = sum(contract(mass_ref[k, j], near[j], 1, 1) for j in range(3))
        weighted_ref[k * size : (k + 1) * size, :] = block.astype(weighted_ref.dtype)


def here():
    snap = lax.axis_index("snap")
    return lax.axis_index("space") * lax.axis_size("snap") + snap, lax.rem(snap, 2)


def chunks_kernel(field_ref, parts_ref, first_ref, sems):
    group, _, length = parts_ref.shape
    own = field_ref.shape[1] // group
    halo = length - own
    copies = []
    copies.append(pltpu.make_async_copy(field_ref.at[:, pl.ds(0, halo)], first_ref, sems.at[group]))
    copies[-1].start()
    for k in range(group):
        start, to, size = k * own - (1 - k % 2) * halo, 0, length
        if k == 0:
            start, to, size = 0, halo, own
        if k == group - 1:
            size = own
        source = field_ref.at[:, pl.ds(start, size)]
        copies.append(pltpu.make_async_copy(source, parts_ref.at[k, :, pl.ds(to, size)], sems.at[k]))
        copies[-1].start()
    for copy in copies:
        copy.wait()


def ends_kernel(before_ref, after_ref, parts_in_ref, parts_ref, sems):
    del parts_in_ref
    group, _, length = parts_ref.shape
    halo = before_ref.shape[1]
    copies = [
        pltpu.make_async_copy(before_ref, parts_ref.at[0, :, pl.ds(0, halo)], sems.at[0]),
        pltpu.make_async_copy(after_ref, parts_ref.at[group - 1, :, pl.ds(length - halo, halo)], sems.at[1]),
    ]
    for copy in copies:
        copy.start()
    for copy in copies:
        copy.wait()


def cut_kernel(field_ref, mass_ref, edge_ref):
    del mass_ref
    width = edge_ref.shape[1]
    core = here()[1]
    edge_ref[...] = field_ref[:, pl.ds(pl.multiple_of((1 - core) * (field_ref.shape[1] - width), width), width)]


def inner_kernel(neighbours_ref, field_ref, mass_ref, weighted_ref, corr_ref, copy_ref, next_ref, block,
                 block_sems, copy_sem):
    count, _, size, _ = mass_ref.shape
    width = STEP * size
    groups = count // STEP
    device, core = here()
    shift = device * count - (1 - core) * STEP
    own = pl.ds(pl.multiple_of((1 - core) * width, width), count * size)
    copy = pltpu.make_async_copy(field_ref.at[:, own], copy_ref, copy_sem)
    copy.start()
    next_ref[...] = field_ref[:, pl.ds(pl.multiple_of(core * width + (1 - core) * (groups - 1) * width, width), width)]
    writes = []
    for step in range(groups - 1):
        slot = step % 2
        if len(writes) >= 2:
            writes[-2].wait()
        first = (step + core) * STEP

        def place(k, j):
            return neighbours_ref[j, first + k] - shift

        weigh(place, STEP, mass_ref.at[pl.ds(first, STEP)], field_ref, block.at[slot], size)
        rows = pl.ds(pl.multiple_of(first * size, width), width)
        writes.append(pltpu.make_async_copy(block.at[slot], weighted_ref.at[rows], block_sems.at[slot]))
        writes[-1].start()
        term = contract(field_ref[:, (step + 1) * width : (step + 2) * width], block[slot], 1, 0)
        corr_ref[...] = term if step == 0 else corr_ref[...] + term
    writes[-2].wait()
    writes[-1].wait()
    copy.wait()


def edge_kernel(neighbours_ref, edge_ref, next_ref, near_ref, mass_ref, corr_in_ref, weighted_in_ref, weighted_ref,
                keep_ref, send_ref, extended, block, block_sem, corr):
    del weighted_in_ref
    count, _, size, _ = mass_ref.shape
    width = STEP * size
    device, core = here()
    first = (1 - core) * (count - STEP)
    extended[:, width : 2 * width] = edge_ref[...]

    @pl.when(core == 0)
    def _():
        extended[:, :width] = next_ref[...]
        extended[:, 2 * width :] = near_ref[...]

    @pl.when(core != 0)
    def _():
        extended[:, :width] = near_ref[...]
        extended[:, 2 * width :] = next_ref[...]

    def place(k, j):
        return neighbours_ref[j, first + k] - device * count - first + HB

    weigh(place, STEP, mass_ref.at[pl.ds(first, STEP)], extended, block, size)
    rows = pl.ds(pl.multiple_of(first * size, width), width)
    write = pltpu.make_async_copy(block, weighted_ref.at[rows], block_sem)
    write.start()
    corr[...] = (corr_in_ref[...] + contract(edge_ref[...], block[...], 1, 0)).T
    tile = keep_ref.shape[1]
    for k in range(keep_ref.shape[0]):
        keep_ref[k] = corr[pl.ds(pl.multiple_of((2 * k + core) * tile, tile), tile), :]
        send_ref[k] = corr[pl.ds(pl.multiple_of((2 * k + 1 - core) * tile, tile), tile), :]
    write.wait()


def pack_kernel(parts_ref, packed_ref):
    total = parts_ref[0]
    for k in range(1, parts_ref.shape[0]):
        total = total + parts_ref[k]
    high, lanes = packed_ref.shape[1:]
    tile = total.shape[0]
    share = lanes // tile
    group = lax.broadcasted_iota(jnp.int32, (high, lanes), 1) // tile
    for k in range(packed_ref.shape[0]):
        piece = total[:, k // share * lanes : (k // share + 1) * lanes]
        packed = jnp.zeros((high, lanes), jnp.float32)
        for g in range(share):
            moved = piece[g * high : (g + 1) * high]
            turn = (g - k % share) % share * tile
            if turn:
                moved = pltpu.roll(moved, turn, 1)
            packed = jnp.where(group == g, moved, packed)
        packed_ref[k] = packed


def unpack_kernel(scale, packed_ref, tile_ref):
    total = packed_ref[0]
    for k in range(1, packed_ref.shape[0]):
        total = total + packed_ref[k]
    total = total * scale
    high = packed_ref.shape[1]
    tile = tile_ref.shape[1]
    share = packed_ref.shape[2] // tile
    for g in range(share):
        tile_ref[g * high : (g + 1) * high, :] = total[:, g * tile : (g + 1) * tile]


def modes_kernel(field_ref, vectors_ref, modes_ref):
    modes_ref[...] = contract(vectors_ref[...], field_ref[...], 0, 0).T.astype(modes_ref.dtype)


def flipped(value, mask):
    return lax.ppermute(value, AXES, [(i, i ^ mask) for i in range(lax.axis_size(AXES))])


def shifted(value, axis, distance):
    count = lax.axis_size(axis)
    return lax.ppermute(value, axis, [(i, (i + distance) % count) for i in range(count)])


def call(kernel, name, operands, out_shape, moved, flops=0, apart=(), out_apart=(), scratch=(), limit=24, **more):
    vmem, smem, anywhere = (pl.BlockSpec(memory_space=m) for m in (pltpu.VMEM, pltpu.SMEM, pl.ANY))
    specs = [smem if x.dtype == jnp.int32 else anywhere if k in apart else vmem for k, x in enumerate(operands)]
    return pl.pallas_call(
        kernel,
        in_specs=specs,
        out_specs=[anywhere if k in out_apart else vmem for k in range(len(out_shape))],
        out_shape=out_shape,
        scratch_shapes=scratch,
        compiler_params=pltpu.CompilerParams(vmem_limit_bytes=limit * MIB),
        cost_estimate=pl.CostEstimate(flops=flops, bytes_accessed=moved, transcendentals=0),
        name=name,
        **more,
    )(*operands)


def shards(snapshots, mass_blocks, neighbours, eigvecs):
    cells, mine = snapshots.shape
    group = lax.axis_size("snap")
    spaces = lax.axis_size("space")
    rows = cells // group
    snaps = mine * group
    size = mass_blocks.shape[2]
    width = STEP * size
    modes_count = eigvecs.shape[1]

    def half(*dims):
        return jax.ShapeDtypeStruct(dims, jnp.bfloat16)

    def single(*dims):
        return jax.ShapeDtypeStruct(dims, jnp.float32)

    sems = pltpu.SemaphoreType.DMA
    flat = snapshots.T
    before = shifted(flat[:, cells - width :], "space", 1)
    chunked = [half(group, mine, rows + width)]
    parts, first = call(
        chunks_kernel,
        "chunks",
        (flat,),
        chunked + [half(mine, width)],
        8 * MIB,
        apart=(0,),
        out_apart=(0, 1),
        scratch=[sems((group + 1,))],
    )
    after = shifted(first, "space", -1)
    (parts,) = call(
        ends_kernel,
        "ends",
        (before, after, parts),
        chunked,
        MIB // 16,
        apart=(0, 1, 2),
        out_apart=(0,),
        scratch=[sems((2,))],
        input_output_aliases={2: 0},
    )
    field = lax.all_to_all(parts, "snap", split_axis=0, concat_axis=0).reshape(snaps, rows + width)
    listed = neighbours.T
    per_row = 2 * snaps * (3 * size + snaps)
    (edge,) = call(cut_kernel, "cut", (field, mass_blocks), [half(snaps, width)], MIB)
    near = flipped(edge, 1)
    weighted, corr, field, following = call(
        inner_kernel,
        "inner",
        (listed, field, mass_blocks),
        [half(rows, snaps), single(snaps, snaps), half(snaps, rows)] + [half(snaps, width)],
        14 * MIB,
        (rows - width) * per_row,
        out_apart=(0, 2),
        scratch=[pltpu.VMEM((2, width, snaps), jnp.bfloat16), sems((2,)), sems(())],
    )
    modes = pl.pallas_call(
        modes_kernel,
        grid=(rows // 1024,),
        in_specs=[
            pl.BlockSpec((snaps, 1024), lambda i: (0, i)),
            pl.BlockSpec((snaps, modes_count), lambda i: (0, 0)),
        ],
        out_specs=pl.BlockSpec((1024, modes_count), lambda i: (i, 0)),
        out_shape=half(rows, modes_count),
        compiler_params=pltpu.CompilerParams(vmem_limit_bytes=16 * MIB),
        cost_estimate=pl.CostEstimate(flops=2 * rows * snaps * modes_count, bytes_accessed=5 * MIB, transcendentals=0),
        name="modes",
    )(field, eigvecs)
    weighted, keep, send = call(
        edge_kernel,
        "edge",
        (listed, edge, following, near, mass_blocks, corr, weighted),
        [half(rows, snaps)] + [single(group // 2, mine, snaps)] * 2,
        6 * MIB,
        width * per_row,
        apart=(6,),
        out_apart=(0,),
        scratch=[
            pltpu.VMEM((snaps, 3 * width), jnp.bfloat16),
            pltpu.VMEM((width, snaps), jnp.bfloat16),
            sems(()),
            pltpu.VMEM((snaps, snaps), jnp.float32),
        ],
        input_output_aliases={6: 0},
    )

    summed = keep + flipped(send, 1)
    chips = [[2 * k + core for k in range(group // 2)] for core in range(2)]
    summed = lax.all_to_all(summed, "snap", split_axis=0, concat_axis=0, axis_index_groups=chips)
    tile = snaps // spaces
    (packed,) = call(pack_kernel, "pack", (summed,), [single(spaces, mine * tile // 128, 128)], MIB)
    packed = lax.all_to_all(packed, "space", split_axis=0, concat_axis=0)
    scale = 1.0 / (rows * lax.axis_size(AXES))
    (correlation,) = call(functools.partial(unpack_kernel, scale), "unpack", (packed,), [single(mine, tile)], MIB)
    return weighted, correlation, modes


def solution(mesh):
    in_specs = (
        P("space", "snap"),
        P(AXES, None, None, None),
        P(AXES, None),
        P(),
    )
    out_specs = (P(AXES, None), P("snap", "space"), P(AXES, None))
    return jax.shard_map(shards, mesh=mesh, in_specs=in_specs, out_specs=out_specs, check_vma=False)
```
